32 devices in a mesh: groups: 1, dp: 16 (over z, y, core), tp: 2 (over x).
Axes of the slice: x: 2, y: 2, z: 4, core: 2. Of those that a mesh axis runs over, the one named last changes fastest.
Arguments:
- latent_cache: bfloat16 [32, 32, 576], P(('groups', 'dp')), may hold values from -6 to 6
- lengths: int32 [32], P('groups'), may hold values from 2 to 30
- destination: int32 [32], P('groups'), may hold values from 0 to 15, as said below
- queries: bfloat16 [32, 2, 64, 576], P(('groups', 'dp'), None, 'tp'), may hold values from -21 to 21
- new_latent: bfloat16 [32, 2, 576], P(('groups', 'dp')), may hold values from -6 to 6
- residual: bfloat16 [32, 2, 3584], P('groups', None, 'dp'), may hold values from -4 to 4
- w_out: bfloat16 [64, 512, 3584], P('tp', None, 'dp'), may hold values from -0.09375 to 0.09375
- norm_gain: float32 [3584], replicated, may hold values from 0.1 to 1.9
- w_gate: bfloat16 [16, 3584, 1024], P('dp', None, 'tp'), may hold values from -0.09375 to 0.09375
- w_up: bfloat16 [16, 3584, 1024], P('dp', None, 'tp'), may hold values from -0.09375 to 0.09375
- w_down: bfloat16 [16, 1024, 3584], P('dp', 'tp'), may hold values from -0.1875 to 0.1875
- experts: int32 [32, 2, 8], P('groups'), may hold values from 0 to 15, all different within a row; in each aligned block of 4 rows (0 to 3, 4 to 7, ..., all dimensions but the last counted through in order) at most 4 rows name the same one
- gate_weights: float32 [32, 2, 8], P('groups'), may hold values from 0.05 to 0.5
Outputs:
- layer_out: bfloat16 [32, 2, 3584], P('groups', None, ('dp', 'tp'))
The draws below stay inside these ranges and needn't reach their ends.
Inputs may be any that keep to these rules, and one draw needn't show every extreme that they name: `destination`: A request keeps its slot index. For each slot index the destinations of the 16 ranks' requests are a permutation of the ranks; no rank sends more than 1 request to one rank, and some rank sends exactly 1 to one rank. Each token names 8 different experts. In the rows of one rank (2 requests times 2 steps, in order) no expert is named more than 4 times, a bound that some block reaches.
All inputs are finite; a program needn't handle non-finite values.
Results may differ from the reference program's by a relative error of at most 0.014.
Values may be sent and summed in bfloat16 or wider, within the bound.
No kernel may reach another device: no remote copies, remote signals or barrier semaphores. Data moves between devices by JAX's collectives and lax.ppermute only.
A program may use at most 128 MiB of HBM per device.

```python
import math
import jax
import jax.numpy as jnp
import numpy as np
from jax import lax

D = 3584
LAT = 512
ROPE = 64
H = 64
FF = 1024
STEPS = 2
SLOTS = 2
CTX = 32
EXPERTS = 16
TOPK = 8
CAP_E = 4
MOVE_CAP = 1
N_DP = 16
N_TP = 2


def draw_latent_cache(key, part):
    key = jax.random.fold_in(key, 11)
    first_key = jax.random.fold_in(key, 0)
    values = jax.random.normal(first_key, (N_DP * SLOTS, CTX, LAT + ROPE), jnp.float32)
    return jnp.clip(values, -6.0, 6.0).astype(jnp.bfloat16)


def draw_queries(key, part):
    key = jax.random.fold_in(key, 12)
    first_key = jax.random.fold_in(key, 0)
    values = jnp.clip(jax.random.normal(first_key, (N_DP * SLOTS, STEPS, H, LAT + ROPE), jnp.float32), -6.0, 6.0)
    return jnp.clip(values, -21.0, 21.0).astype(jnp.bfloat16)


def draw_destination(key, part):
    key = jax.random.fold_in(key, 13)
    first_key, second_key = jax.random.split(key)
    ranking = jax.random.permutation(first_key, N_DP).astype(jnp.int32)
    inverse = jnp.zeros((N_DP,), jnp.int32).at[ranking].set(jnp.arange(N_DP, dtype=jnp.int32))
    offsets = jax.random.permutation(second_key, N_DP * MOVE_CAP).astype(jnp.int32)[:SLOTS] % N_DP
    targets = inverse[(ranking[:, None] + offsets[None, :]) % N_DP]
    return targets.reshape(N_DP * SLOTS).astype(jnp.int32)


def touch_ends(result, rng, low, top_value):
    place = [jax.random.randint(jax.random.fold_in(rng, axis), (), 0, length) for axis, length in enumerate(result.shape)]
    longest = result.shape.index(max(result.shape))
    beside = place[:longest] + [(place[longest] + 1) % result.shape[longest]] + place[longest + 1:]
    return result.at[tuple(place)].set(low).at[tuple(beside)].set(top_value)


def block_scale(rng, extent, shards, low, high):
    gain, own = 1.0, jax.random.fold_in(rng, 6)
    for position, blocks in shards:
        steps = jnp.exp(jax.random.uniform(jax.random.fold_in(own, position), (blocks,), jnp.float32, low / len(shards), high / len(shards)))
        gain = gain * jnp.repeat(steps, extent[position] // blocks).reshape([-1 if axis == position else 1 for axis in range(len(extent))])
    return gain


def shared_out(key, own, number, rows, count, top, reach, slope):
    order = jax.random.permutation(key, count)
    packed, usual = shares(count, rows * top, reach, slope, True), shares(count, rows * top, reach, slope, False)
    places = jnp.arange(count)

    def named(sizes, offset_by):
        used = int((sizes > 0).sum())
        fixed = max(1, used // 4)
        moved = fixed + (places - fixed + offset_by * (used - fixed)) % max(1, count - fixed)
        return jnp.zeros((count,), jnp.int32).at[order[jnp.where(places < fixed, places, moved)]].set(jnp.asarray(sizes, jnp.int32))

    sizes = jnp.where(number % 4 == 0, named(packed, number // 4), named(usual, number - number // 4 - 1))
    mixed = jax.random.permutation(jax.random.fold_in(own, 3), count)
    donor, sink = mixed[0:count // 2 * 2:2], mixed[1:count // 2 * 2:2]
    margin = jnp.minimum(sizes[donor] - 1, reach - sizes[sink]) // 2
    margin = jnp.where((donor == order[0]) | (sink == order[0]) | (sizes[sink] == 0), 0, jnp.maximum(margin, 0))
    moved = jax.random.randint(jax.random.fold_in(own, 4), (count // 2,), 0, 1 << 20) % (margin + 1)
    sizes = sizes.at[donor].add(-moved).at[sink].add(moved)
    labels = jnp.searchsorted(jnp.cumsum(sizes), jnp.arange(rows * top), side="right").astype(jnp.int32)
    grid = labels.reshape(top, rows).T
    grid = grid[jax.random.permutation(jax.random.fold_in(own, 1), rows)]
    offset_by = jax.random.randint(jax.random.fold_in(own, 2), (rows, 1), 0, top)
    return jnp.take_along_axis(grid, (jnp.arange(top)[None, :] + offset_by) % top, axis=1)


def shares(count, total, reach, lean, full):
    weights = [(1 << 20) // math.isqrt(grade ** lean) + 1 for grade in range(1, count + 1)]
    largest = reach if full else min(reach, max(-(-total // count), total * weights[0] // sum(weights)))
    least = 1 if total - largest >= count - 1 else 0
    holding, surplus = [largest] + [least] * (count - 1), total - largest - least * (count - 1)
    while surplus > 0:
        free = [i for i in range(1, count) if holding[i] < largest] or [i for i in range(1, count) if holding[i] < reach]
        whole, budget = sum([weights[i] for i in free]), surplus
        for i in free:
            more = min(reach - holding[i], max(1, budget * weights[i] // whole), surplus)
            holding[i] = holding[i] + more
            surplus = surplus - more
    return np.array(holding)


def centred(own_key, dims, scale, most, cuts=(), held_as=jnp.bfloat16):
    result = jax.random.normal(own_key, dims, jnp.float32) * scale
    if len(cuts) > 0:
        result = block_scale(own_key, dims, cuts, -0.22, 0.18) * result
    return jnp.clip(result, min=-most, max=most).astype(held_as)


def setup_inputs(seed: int = 0, part: int = 0) -> dict:
    streams_of = jax.random.split(jax.random.key(seed), 14)
    part_splits = jax.random.split(jax.random.fold_in(streams_of[13], part), 14)
    latent_cache = draw_latent_cache(jax.random.fold_in(jax.random.fold_in(streams_of[13], part), 71), part)
    lengths = touch_ends(jax.random.randint(part_splits[1], (N_DP * SLOTS,), 2, CTX - 1), jax.random.fold_in(part_splits[1], 1), 2, (CTX - 1) - 1).astype(jnp.int32)
    destination = draw_destination(jax.random.fold_in(jax.random.fold_in(streams_of[13], part), 71), part)
    queries = draw_queries(jax.random.fold_in(jax.random.fold_in(streams_of[13], part), 71), part)
    new_latent = centred(part_splits[4], (N_DP * SLOTS, STEPS, LAT + ROPE), 1.0, 6.0, ((0, 16),))
    residual = centred(part_splits[5], (N_DP * SLOTS, STEPS, D), 0.5, 4.0, ((2, 16),))
    w_out = centred(streams_of[6], (H, LAT, D), (H * LAT // 8) ** -0.5, 0.09375, ((0, 2), (2, 16)))
    norm_gain = jnp.clip(1.0 + 0.18 * jax.random.normal(streams_of[7], (D,), jnp.float32), 0.1, 1.9)
    w_gate = centred(streams_of[8], (EXPERTS, D, FF), D ** -0.5, 0.09375, ((0, 16), (2, 2)))
    w_up = centred(streams_of[9], (EXPERTS, D, FF), D ** -0.5, 0.09375, ((0, 16), (2, 2)))
    w_down = centred(streams_of[10], (EXPERTS, FF, D), FF ** -0.5, 0.1875, ((0, 16), (1, 2)))
    experts_keys = jax.random.split(jax.random.fold_in(part_splits[11], 1), (N_DP * SLOTS) * STEPS // (SLOTS * STEPS))
    experts_turns = jax.random.permutation(jax.random.fold_in(part_splits[11], 3), (N_DP * SLOTS) * STEPS // (SLOTS * STEPS))
    experts = jax.vmap(lambda own, number: shared_out(jax.random.fold_in(part_splits[11], 2), own, number, SLOTS * STEPS, EXPERTS, TOPK, CAP_E, 2))(experts_keys, experts_turns).reshape((N_DP * SLOTS, STEPS, TOPK))
    gate_weights = jnp.clip(jnp.exp(jax.random.uniform(part_splits[12], (N_DP * SLOTS, STEPS, TOPK), jnp.float32, math.log(0.05), math.log(0.5))), 0.05, 0.5)
    return dict(latent_cache=latent_cache, lengths=lengths, destination=destination, queries=queries, new_latent=new_latent, residual=residual, w_out=w_out, norm_gain=norm_gain, w_gate=w_gate, w_up=w_up, w_down=w_down, experts=experts, gate_weights=gate_weights)


score_scale = 192.0 ** (-0.5)
norm_eps = 1e-06

def expert_slots(experts, block_count, expert_count, capacity):
    flat_ids = experts.reshape(block_count, -1)
    onehot = (flat_ids[:, :, None] == jnp.arange(expert_count, dtype=jnp.int32)[None, None, :]).astype(jnp.int32)
    before = jnp.cumsum(onehot, axis=1) - onehot
    within = lax.optimization_barrier(jnp.sum(onehot * before, axis=-1))
    position_in = jnp.arange(block_count, dtype=jnp.int32)[:, None] * capacity + within
    return (position_in.reshape(-1), flat_ids.reshape(-1))

def reference(latent_cache, lengths, destination, queries, new_latent, residual, w_out, norm_gain, w_gate, w_up, w_down, experts, gate_weights):
    slot_range = jnp.tile(jnp.arange(SLOTS, dtype=jnp.int32), N_DP)
    target = destination * SLOTS + slot_range
    moved = jnp.zeros_like(latent_cache).at[target].set(latent_cache)
    moved_len = jnp.zeros_like(lengths).at[target].set(lengths)
    position_range = jnp.arange(CTX, dtype=jnp.int32)
    full_cache = moved
    for step_index in range(STEPS):
        writing = position_range[None, :] == (moved_len + step_index)[:, None]
        full_cache = jnp.where(writing[:, :, None], new_latent[:, step_index][:, None, :], full_cache)
    visible = position_range[None, None, :] < (moved_len[:, None] + jnp.arange(STEPS, dtype=jnp.int32)[None, :] + 1)[:, :, None]
    cache_wide = full_cache.astype(jnp.float32)
    scores = jnp.einsum('gtha,gpa->gthp', queries.astype(jnp.float32), cache_wide) * score_scale
    scores = jnp.where(visible[:, :, None, :], scores, -1e+30)
    highest = lax.optimization_barrier(jnp.max(scores, axis=-1, keepdims=True))
    raised = jnp.exp(scores - highest)
    weights = (raised / lax.optimization_barrier(jnp.sum(raised, axis=-1, keepdims=True))).astype(jnp.bfloat16)
    weights = lax.optimization_barrier(weights).astype(jnp.float32)
    attended = jnp.einsum('gthp,gpl->gthl', weights, cache_wide[..., :LAT]).astype(jnp.bfloat16)
    row_total = N_DP * SLOTS * STEPS
    attn_out = jnp.dot(attended.reshape(row_total, H * LAT), w_out.reshape(H * LAT, D), preferred_element_type=jnp.float32)
    mixed = (residual.reshape(row_total, D).astype(jnp.float32) + attn_out).astype(jnp.bfloat16)
    mixed_wide = mixed.astype(jnp.float32)
    normed = (mixed_wide * lax.rsqrt(lax.optimization_barrier(jnp.mean(mixed_wide * mixed_wide, axis=-1, keepdims=True)) + norm_eps) * norm_gain).astype(jnp.bfloat16)
    slot_room = N_DP * CAP_E
    position_in, expert_flat = expert_slots(experts, N_DP, EXPERTS, CAP_E)
    row_ids = jnp.arange(row_total * TOPK, dtype=jnp.int32) // TOPK
    sender_table = jnp.full((EXPERTS * slot_room,), -1, jnp.int32).at[expert_flat * slot_room + position_in].set(row_ids)
    dispatched = jnp.where((sender_table >= 0)[:, None], normed[jnp.maximum(sender_table, 0)], 0)
    dispatched = dispatched.reshape(EXPERTS, slot_room, D)

    def one_expert(operands):
        rows_in, gate_matrix, up_matrix, down_matrix = operands
        gate_proj = jnp.dot(rows_in, gate_matrix, preferred_element_type=jnp.float32)
        up_proj = jnp.dot(rows_in, up_matrix, preferred_element_type=jnp.float32)
        activated = (jax.nn.silu(gate_proj) * up_proj).astype(jnp.bfloat16)
        activated = lax.optimization_barrier(activated).astype(jnp.float32)
        block_terms = jnp.einsum('snf,nfd->snd', activated.reshape(slot_room, N_TP, FF // N_TP), down_matrix.astype(jnp.float32).reshape(N_TP, FF // N_TP, D))
        block_terms = lax.optimization_barrier(block_terms.astype(jnp.bfloat16)).astype(jnp.float32)
        return lax.optimization_barrier(jnp.sum(block_terms, axis=1))
    outputs = lax.map(one_expert, (dispatched, w_gate, w_up, w_down))
    picked = outputs.reshape(EXPERTS * slot_room, D)[expert_flat * slot_room + position_in].reshape(row_total, TOPK, D)
    moe_part = lax.optimization_barrier(jnp.sum(gate_weights.reshape(row_total, TOPK)[:, :, None] * picked, axis=1))
    return (mixed_wide + moe_part).astype(jnp.bfloat16).reshape(N_DP * SLOTS, STEPS, D)
```

```python
import jax
import jax.numpy as jnp
from jax import lax
from jax.sharding import Mesh, PartitionSpec as P

score_scale = 192.0 ** (-0.5)
norm_eps = 1e-06


def swap_core(x):
    return lax.ppermute(x, "core", [(0, 1), (1, 0)])


def swap_chip(x, bits):
    count = lax.axis_size("chip")
    return lax.ppermute(x, "chip", [(i, i ^ bits) for i in range(count)])


def swap_tp(x, bits):
    count = lax.axis_size("tp")
    return lax.ppermute(x, "tp", [(i, i ^ bits) for i in range(count)])


def gather_relative(x):
    chips = lax.axis_size("chip")
    far = jnp.stack([x] + [swap_chip(x, 2 * k) for k in range(1, chips // 2)])
    near = jnp.stack([far, swap_chip(far, 1)])
    return jnp.stack([near, swap_core(near)])


def gather_equal(x, axes, count):
    spread = jnp.broadcast_to(x[None], (count,) + x.shape)
    return lax.all_to_all(spread, axes, 0, 0, tiled=True)


def body(
    latent_cache,
    lengths,
    destination,
    queries,
    new_latent,
    residual,
    w_out,
    norm_gain,
    w_gate,
    w_up,
    w_down,
    experts,
    gate_weights,
):
    chips = lax.axis_size("chip")
    tp_width = lax.axis_size("tp")
    ranks = chips * 2
    chip_here = lax.axis_index("chip")
    core_here = lax.axis_index("core")
    tp_here = lax.axis_index("tp")
    rank_here = chip_here * 2 + core_here
    slot_count, positions, latent_all = latent_cache.shape
    heads_here, latent_width, column_count = w_out.shape
    step_count = queries.shape[1]
    block_rows = slot_count * step_count
    row_total = ranks * block_rows

    everyone = gather_relative(latent_cache)
    everyone = everyone.reshape(ranks * slot_count, positions, latent_all)
    slots = jnp.tile(jnp.arange(slot_count, dtype=jnp.int32), ranks)
    request = jnp.arange(ranks * slot_count, dtype=jnp.int32)
    goes_to = destination * slot_count + slots
    source = jnp.sum(
        jnp.where(goes_to[None, :] == request[:, None], request[None, :], 0), axis=1
    )
    moved_len = jnp.sum(
        jnp.where(goes_to[None, :] == request[:, None], lengths[None, :], 0), axis=1
    )
    relative = (source // slot_count) ^ rank_here
    place = (
        ((relative & 1) * chips + ((relative >> 1) & 1) * (chips // 2) + (relative >> 2))
        * slot_count
        + source % slot_count
    )
    moved = everyone[place]
    position_range = jnp.arange(positions, dtype=jnp.int32)

    def inserted(base, fresh, length):
        for step_index in range(step_count):
            writing = position_range[None, :] == (length + step_index)[:, None]
            base = jnp.where(writing[:, :, None], fresh[:, step_index][:, None, :], base)
        return base

    own_first = rank_here * slot_count
    own_len = lax.dynamic_slice_in_dim(moved_len, own_first, slot_count, 0)
    own_cache = inserted(
        lax.dynamic_slice_in_dim(moved, own_first, slot_count, 0), new_latent, own_len
    )
    visible = (
        position_range[None, None, :]
        < (own_len[:, None] + jnp.arange(step_count, dtype=jnp.int32)[None, :] + 1)[:, :, None]
    )
    scores = (
        jnp.einsum("stha,spa->sthp", queries, own_cache, preferred_element_type=jnp.float32)
        * score_scale
    )
    scores = jnp.where(visible[:, :, None, :], scores, -1e30)
    highest = jnp.max(scores, axis=-1, keepdims=True)
    raised = jnp.exp(scores - highest)
    weights = (raised / jnp.sum(raised, axis=-1, keepdims=True)).astype(jnp.bfloat16)

    weight_count = block_rows * heads_here * positions
    fresh_count = block_rows * latent_width
    lane = 128
    sent = jnp.concatenate(
        [
            weights.reshape(weight_count // lane, lane),
            new_latent[..., :latent_width].reshape(fresh_count // lane, lane),
        ]
    )
    arrived = gather_equal(sent, ("chip", "core"), ranks)
    all_weights = arrived[:, : weight_count // lane].reshape(
        ranks * slot_count, step_count, heads_here, positions
    )
    all_fresh = arrived[:, weight_count // lane :].reshape(
        ranks * slot_count, step_count, latent_width
    )
    all_cache = inserted(moved[..., :latent_width], all_fresh, moved_len)
    attended = jnp.einsum(
        "gthp,gpl->gthl", all_weights, all_cache, preferred_element_type=jnp.float32
    ).astype(jnp.bfloat16)
    head_partial = jnp.dot(
        attended.reshape(row_total, heads_here * latent_width),
        w_out.reshape(heads_here * latent_width, column_count),
        preferred_element_type=jnp.float32,
    ).astype(jnp.bfloat16)
    attn_cols = head_partial.astype(jnp.float32)
    for k in range(1, tp_width):
        attn_cols = attn_cols + swap_tp(head_partial, k).astype(jnp.float32)
    mixed = (residual.reshape(row_total, column_count).astype(jnp.float32) + attn_cols).astype(
        jnp.bfloat16
    )

    same_core = gather_equal(mixed, "chip", chips)
    other_core = swap_core(same_core)
    first = jnp.where(core_here == 0, same_core, other_core)
    second = jnp.where(core_here == 0, other_core, same_core)
    rows_in = jnp.stack([first, second], axis=1).transpose(2, 0, 1, 3).reshape(row_total, -1)
    rows_wide = rows_in.astype(jnp.float32)
    inverse_rms = lax.rsqrt(jnp.mean(rows_wide * rows_wide, axis=-1, keepdims=True) + norm_eps)
    normed = (rows_wide * inverse_rms * norm_gain).astype(jnp.bfloat16)
    gate_proj = jnp.dot(normed, w_gate[0], preferred_element_type=jnp.float32)
    up_proj = jnp.dot(normed, w_up[0], preferred_element_type=jnp.float32)
    activated = (jax.nn.silu(gate_proj) * up_proj).astype(jnp.bfloat16)
    expert_terms = jnp.dot(activated, w_down[0], preferred_element_type=jnp.float32)
    top_count = experts.shape[2]
    own_gate = jnp.sum(
        jnp.where(experts == rank_here, gate_weights, 0.0).reshape(row_total, top_count), axis=1
    )
    share = column_count // tp_width
    terms = (
        (expert_terms * own_gate[:, None])
        .astype(jnp.bfloat16)
        .reshape(row_total, chips, 2, tp_width * share)
        .transpose(2, 1, 0, 3)
    )
    mine = lax.dynamic_index_in_dim(terms, core_here, 0, keepdims=False)
    theirs = lax.dynamic_index_in_dim(terms, 1 - core_here, 0, keepdims=False)
    chip_sum = (mine.astype(jnp.float32) + swap_core(theirs).astype(jnp.float32)).astype(
        jnp.bfloat16
    )
    leaving = (
        chip_sum.reshape(chips, row_total, tp_width, share)
        .transpose(0, 2, 1, 3)
        .reshape(chips * tp_width, row_total, share)
    )
    returned = lax.all_to_all(leaving, ("chip", "tp"), 0, 0, tiled=True)
    moe_part = jnp.sum(returned.astype(jnp.float32), axis=0)
    own_columns = lax.dynamic_slice_in_dim(mixed, tp_here * share, share, 1)
    return (
        (own_columns.astype(jnp.float32) + moe_part)
        .astype(jnp.bfloat16)
        .reshape(residual.shape[0], step_count, share)
    )


def solution(mesh):
    groups, ranks, tp_width = (mesh.shape[name] for name in ("groups", "dp", "tp"))
    split = Mesh(
        mesh.devices.reshape(groups, ranks // 2, 2, tp_width), ("groups", "chip", "core", "tp")
    )
    dp = ("chip", "core")
    placed = (
        P(("groups",) + dp, None, None),
        P("groups"),
        P("groups"),
        P(("groups",) + dp, None, "tp", None),
        P(("groups",) + dp, None, None),
        P("groups", None, dp),
        P("tp", None, dp),
        P(),
        P(dp, None, "tp"),
        P(dp, None, "tp"),
        P(dp, "tp", None),
        P("groups", None, None),
        P("groups", None, None),
    )
    return jax.shard_map(
        body,
        mesh=split,
        in_specs=placed,
        out_specs=P("groups", None, dp + ("tp",)),
        check_vma=False,
    )
```

```python
import jax
import jax.numpy as jnp
from jax import lax
from jax.experimental import pallas as pl
from jax.experimental.pallas import tpu as pltpu
from jax.sharding import Mesh, PartitionSpec as P

score_scale = 192.0 ** (-0.5)
norm_eps = 1e-06


def swap_core(x):
    return lax.ppermute(x, "core", [(0, 1), (1, 0)])


def swap_chip(x, bits):
    count = lax.axis_size("chip")
    return lax.ppermute(x, "chip", [(i, i ^ bits) for i in range(count)])


def swap_tp(x, bits):
    count = lax.axis_size("tp")
    return lax.ppermute(x, "tp", [(i, i ^ bits) for i in range(count)])


def gather_relative(x):
    chips = lax.axis_size("chip")
    far = [x] + [swap_chip(x, 2 * k) for k in range(1, chips // 2)]
    near = [swap_chip(x, 1)]
    for arrived in far[1:]:
        near.append(swap_chip(arrived, 1))
    return far + near + [swap_core(part) for part in far + near]


def nt_dot(a, b):
    return lax.dot_general(a, b, (((1,), (1,)), ((), ())), preferred_element_type=jnp.float32)


def inserted_rows(base, fresh, length):
    position = lax.broadcasted_iota(jnp.int32, base.shape, 0)
    for step_index, row in enumerate(fresh):
        base = jnp.where(position == length + step_index, row, base)
    return base


def bring_kernel(*refs):
    count = len(refs) // 2
    copies = [
        pltpu.make_async_copy(refs[k], refs[count + k], refs[-1].at[k]) for k in range(count)
    ]
    for copy in copies:
        copy.start()
    for copy in copies:
        copy.wait()


def weigh_kernel(table, *refs):
    parts, (queries, new_latent, out, held, sems) = refs[:-5], refs[-5:]
    slot_count, positions, _ = held.shape
    step_count, heads, _ = queries.shape[1:]
    width = out.shape[1]
    requests = (table.shape[0] - 1) // 2
    rank = table[2 * requests]
    for s in range(slot_count):
        part = table[rank * slot_count + s] // slot_count
        for k, ref in enumerate(parts):

            @pl.when(part == k)
            def _():
                pltpu.make_async_copy(ref.at[s], held.at[s], sems.at[s]).start()

    slabs = []
    for s in range(slot_count):
        length = table[requests + rank * slot_count + s]
        pltpu.make_async_copy(parts[0].at[s], held.at[s], sems.at[s]).wait()
        fresh = [new_latent[s, t : t + 1, :].astype(jnp.float32) for t in range(step_count)]
        keys = inserted_rows(held[s].astype(jnp.float32), fresh, length).astype(jnp.bfloat16)
        rows = queries[s].reshape(step_count * heads, keys.shape[1])
        scores = nt_dot(rows, keys) * score_scale
        step_of = lax.broadcasted_iota(jnp.int32, scores.shape, 0) // heads
        position = lax.broadcasted_iota(jnp.int32, scores.shape, 1)
        scores = jnp.where(position < length + step_of + 1, scores, -1e30)
        raised = jnp.exp(scores - jnp.max(scores, axis=-1, keepdims=True))
        weights = raised / jnp.sum(raised, axis=-1, keepdims=True)
        slabs += [weights[k * 8 : (k + 1) * 8] for k in range(step_count * heads // 8)]
    top = jnp.concatenate(slabs, axis=1)
    row = lax.broadcasted_iota(jnp.int32, (8, width), 0)
    bottom = jnp.zeros((8, width), jnp.float32)
    for s in range(slot_count):
        for t in range(step_count):
            bottom = jnp.where(
                row == s * step_count + t,
                new_latent[s, t : t + 1, :width].astype(jnp.float32),
                bottom,
            )
    out[...] = jnp.concatenate([top, bottom], axis=0).astype(out.dtype)


def project_kernel(table, *refs):
    parts, rest = refs[:-16], refs[-16:]
    sent_same, sent_other, w_out = rest[:3]
    sources, out, targets = rest[3:6], rest[6], rest[7:10]
    caches, wide, keys, attended, sems, load_sems = rest[10:]
    requests, positions, _ = caches.shape
    heads, columns, latent_width = w_out.shape
    chips = sent_same.shape[0]
    slot_count = step_count = 2
    copies = []
    for k, ref in enumerate(parts):
        copies.append(
            pltpu.make_async_copy(
                ref.at[:, :, pl.ds(0, latent_width)],
                caches.at[pl.ds(k * slot_count, slot_count)],
                sems.at[k],
            )
        )
    loads = [
        pltpu.make_async_copy(source, target, load_sems.at[k])
        for k, (source, target) in enumerate(zip(sources, targets))
    ]
    for copy in copies + loads:
        copy.start()
    core = table[2 * requests] % 2
    lanes = 128
    for k, ref in enumerate((sent_same, sent_other)):
        for c in range(chips):
            for g in range(slot_count * step_count):
                wide[k, g, c * 8 : (c + 1) * 8, :] = ref[
                    c, :8, g * lanes : (g + 1) * lanes
                ].astype(jnp.float32)
    per_lane = lanes // positions
    block = chips * positions
    deep = lax.broadcasted_iota(jnp.int32, (lanes, per_lane * block), 0)
    across = lax.broadcasted_iota(jnp.int32, (lanes, per_lane * block), 1)
    spread = (
        (deep // positions == across // block) & (deep % positions == across % positions)
    ).astype(jnp.bfloat16)
    group_rows = 8 * step_count * chips
    row = lax.broadcasted_iota(jnp.int32, (group_rows, per_lane * block), 0)
    lane = lax.broadcasted_iota(jnp.int32, (group_rows, per_lane * block), 1)
    own_block = row % chips == (lane % block) // positions
    for copy in copies:
        copy.wait()
    taken = step_count * chips
    for s in range(slot_count):
        for k in range(2):
            group = s * 2 + k
            for c in range(chips):
                request = (c * 2 + (core ^ k)) * slot_count + s
                length = table[requests + request]
                bottom = (sent_same, sent_other)[k][c, 8:, :].astype(jnp.float32)
                fresh = [
                    bottom[s * step_count + t : s * step_count + t + 1]
                    for t in range(step_count)
                ]
                base = caches[table[request]].astype(jnp.float32)
                keys[c * positions : (c + 1) * positions, :] = inserted_rows(
                    base, fresh, length
                ).astype(jnp.bfloat16)
            rows = [
                wide[k, s * step_count + t, pl.ds(q, chips, stride=8), :]
                for q in range(8)
                for t in range(step_count)
            ]
            packed = jnp.concatenate(rows, axis=0).astype(jnp.bfloat16)
            spaced = jnp.dot(packed, spread, preferred_element_type=jnp.float32)
            spaced = jnp.where(own_block, spaced, 0.0).astype(jnp.bfloat16)
            for r in range(per_lane):
                product = jnp.dot(
                    spaced[:, r * block : (r + 1) * block],
                    keys[...],
                    preferred_element_type=jnp.float32,
                ).astype(jnp.bfloat16)
                for q in range(8):
                    attended[r * 8 + q, group * taken : (group + 1) * taken, :] = product[
                        q * taken : (q + 1) * taken
                    ]
    total = jnp.zeros((attended.shape[1], columns), jnp.float32)
    for h in range(heads):
        total = total + nt_dot(attended[h], w_out[h])
    count = total.shape[0]
    to = lax.broadcasted_iota(jnp.int32, (count, count), 0)
    source = lax.broadcasted_iota(jnp.int32, (count, count), 1)
    core_of, slot_of, step_of = (to // 4) % 2, (to // 2) % 2, to % 2
    relative = jnp.where(core == 0, core_of, 1 - core_of)
    moved = (slot_of * 2 + relative) * taken + step_of * chips + to // 8
    order = (source == moved).astype(jnp.bfloat16)
    out[...] = jnp.dot(
        order, total.astype(jnp.bfloat16), preferred_element_type=jnp.float32
    ).astype(out.dtype)
    for load in loads:
        load.wait()


def expert_kernel(table, same, other, gain, experts, gates, w_gate, w_up, w_down, keep, give):
    chips, rows, columns = same.shape
    features = chips * 2 * columns
    core = table[table.shape[0] - 1] % 2
    squares = jnp.zeros((rows, columns), jnp.float32)
    for ref in (same, other):
        for c in range(chips):
            x = ref[c].astype(jnp.float32)
            squares = squares + x * x
    scale = lax.rsqrt(jnp.sum(squares, axis=1, keepdims=True) / features + norm_eps)
    hidden = w_gate.shape[1]
    gate_proj = jnp.zeros((rows, hidden), jnp.float32)
    up_proj = jnp.zeros((rows, hidden), jnp.float32)
    for k, ref in enumerate((same, other)):
        for c in range(chips):
            block = c * 2 + (core ^ k)
            normed = (ref[c].astype(jnp.float32) * scale * gain[pl.ds(block, 1), :]).astype(
                jnp.bfloat16
            )
            first = pl.multiple_of(block * columns, 32)
            gate_proj += jnp.dot(
                normed, w_gate[pl.ds(first, columns), :], preferred_element_type=jnp.float32
            )
            up_proj += jnp.dot(
                normed, w_up[pl.ds(first, columns), :], preferred_element_type=jnp.float32
            )
    activated = (gate_proj / (1.0 + jnp.exp(-gate_proj)) * up_proj).astype(jnp.bfloat16)
    rank = table[table.shape[0] - 1]
    by_step = jnp.sum(jnp.where(experts[...] == rank, gates[...], 0.0), axis=1)
    steps, requests = by_step.shape
    row = lax.broadcasted_iota(jnp.int32, (rows, requests), 0)
    request = lax.broadcasted_iota(jnp.int32, (rows, requests), 1)
    own_gate = jnp.zeros((rows, 1), jnp.float32)
    for t in range(steps):
        here = request * steps + t == row
        own_gate += jnp.sum(jnp.where(here, by_step[t : t + 1], 0.0), axis=1, keepdims=True)
    share = keep.shape[2]
    tile = 8 * share
    for first in range(0, features, tile):
        terms = own_gate * jnp.dot(
            activated, w_down[:, first : first + tile], preferred_element_type=jnp.float32
        )
        pieces = [terms[:, j * share : (j + 1) * share].astype(keep.dtype) for j in range(8)]

        def put(even, odd):
            for j in range(8):
                target = even if (j // 2) % 2 == 0 else odd
                target[(first // tile) * 4 + (j // 4) * 2 + j % 2] = pieces[j]

        @pl.when(core == 0)
        def _():
            put(keep, give)

        @pl.when(core == 1)
        def _():
            put(give, keep)


VMEM = pl.BlockSpec(memory_space=pltpu.VMEM)
SMEM = pl.BlockSpec(memory_space=pltpu.SMEM)
ANY = pl.BlockSpec(memory_space=pl.ANY)


def in_vmem(x):
    return pltpu.with_memory_space_constraint(x, pltpu.VMEM)


def in_hbm(x):
    return pltpu.with_memory_space_constraint(x, pltpu.HBM)


def bring(*arrays):
    return pl.pallas_call(
        bring_kernel,
        out_shape=[pltpu.VMEM(x.shape, x.dtype) for x in arrays],
        in_specs=[ANY] * len(arrays),
        out_specs=[VMEM] * len(arrays),
        scratch_shapes=[pltpu.SemaphoreType.DMA((len(arrays),))],
        compiler_params=pltpu.CompilerParams(vmem_limit_bytes=2 * 2**20),
        cost_estimate=pl.CostEstimate(
            flops=0, bytes_accessed=sum(2 * x.size * x.dtype.itemsize for x in arrays), transcendentals=0
        ),
        name="bring_to_vmem",
    )(*[in_hbm(x) for x in arrays])


def weigh(table, parts, queries, new_latent, latent_width):
    slot_count, positions, latent_all = parts[0].shape
    return pl.pallas_call(
        weigh_kernel,
        out_shape=jax.ShapeDtypeStruct((16, latent_width), jnp.bfloat16),
        in_specs=[SMEM] + [ANY] * len(parts) + [VMEM] * 2,
        out_specs=VMEM,
        scratch_shapes=[
            pltpu.VMEM((slot_count, positions, latent_all), jnp.bfloat16),
            pltpu.SemaphoreType.DMA((slot_count,)),
        ],
        compiler_params=pltpu.CompilerParams(vmem_limit_bytes=8 * 2**20),
        name="softmax_weights",
    )(table, *parts, in_vmem(queries), in_vmem(new_latent))


def project(table, parts, sent_same, sent_other, w_out, later):
    heads, columns, latent_width = w_out.shape
    slot_count, positions, _ = parts[0].shape
    requests = len(parts) * slot_count
    rows = requests * 2
    return pl.pallas_call(
        project_kernel,
        out_shape=[jax.ShapeDtypeStruct((rows, columns), jnp.bfloat16)]
        + [pltpu.VMEM(x.shape, x.dtype) for x in later],
        in_specs=[SMEM] + [ANY] * len(parts) + [VMEM] * 3 + [ANY] * len(later),
        out_specs=[VMEM] * (1 + len(later)),
        scratch_shapes=[
            pltpu.VMEM((requests, positions, latent_width), jnp.bfloat16),
            pltpu.VMEM((2, 4, sent_same.shape[0] * 8, 128), jnp.float32),
            pltpu.VMEM((sent_same.shape[0] * positions, latent_width), jnp.bfloat16),
            pltpu.VMEM((heads, rows, latent_width), jnp.bfloat16),
            pltpu.SemaphoreType.DMA((len(parts),)),
            pltpu.SemaphoreType.DMA((len(later),)),
        ],
        compiler_params=pltpu.CompilerParams(vmem_limit_bytes=8 * 2**20),
        name="attend_project",
    )(table, *parts, sent_same, sent_other, in_vmem(w_out), *[in_hbm(x) for x in later])


def run_expert(table, same, other, gain, experts, gates, w_gate, w_up, w_down, share):
    chips, rows, _ = same.shape
    shape = jax.ShapeDtypeStruct((chips * 2, rows, share), jnp.bfloat16)
    return pl.pallas_call(
        expert_kernel,
        out_shape=(shape, shape),
        in_specs=[SMEM] + [VMEM] * 8,
        out_specs=(VMEM, VMEM),
        compiler_params=pltpu.CompilerParams(vmem_limit_bytes=8 * 2**20),
        name="expert_mlp",
    )(
        table,
        same,
        other,
        gain,
        experts,
        gates,
        in_vmem(w_gate),
        in_vmem(w_up),
        in_vmem(w_down),
    )


def gather_equal(x, axes, count):
    spread = jnp.broadcast_to(x[None], (count,) + x.shape)
    return lax.all_to_all(spread, axes, 0, 0, tiled=True)


def body(
    latent_cache,
    lengths,
    destination,
    queries,
    new_latent,
    residual,
    w_out,
    norm_gain,
    w_gate,
    w_up,
    w_down,
    experts,
    gate_weights,
):
    chips = lax.axis_size("chip")
    tp_width = lax.axis_size("tp")
    ranks = chips * 2
    chip_here = lax.axis_index("chip")
    core_here = lax.axis_index("core")
    tp_here = lax.axis_index("tp")
    rank_here = chip_here * 2 + core_here
    slot_count, positions, latent_all = latent_cache.shape
    heads_here, latent_width, column_count = w_out.shape
    step_count = queries.shape[1]
    block_rows = slot_count * step_count
    row_total = ranks * block_rows

    with_kernels = (
        slot_count == 2
        and step_count == 2
        and chips == 8
        and tp_width == 2
        and (positions, heads_here, latent_width, column_count) == (32, 32, 512, 224)
    )
    parts = gather_relative(latent_cache)
    slots = jnp.tile(jnp.arange(slot_count, dtype=jnp.int32), ranks)
    request = jnp.arange(ranks * slot_count, dtype=jnp.int32)
    goes_to = destination * slot_count + slots
    source = jnp.sum(
        jnp.where(goes_to[None, :] == request[:, None], request[None, :], 0), axis=1
    )
    moved_len = jnp.sum(
        jnp.where(goes_to[None, :] == request[:, None], lengths[None, :], 0), axis=1
    )
    relative = (source // slot_count) ^ rank_here
    place = (
        ((relative & 1) * chips + ((relative >> 1) & 1) * (chips // 2) + (relative >> 2))
        * slot_count
        + source % slot_count
    )
    own_gate = jnp.sum(jnp.where(experts == rank_here, gate_weights, 0.0), axis=2).reshape(
        row_total, 1
    )
    share = column_count // tp_width
    first_column = tp_here * share
    residual_rows = residual.reshape(row_total, column_count)
    gain_rows = norm_gain.reshape(ranks, column_count)
    if with_kernels:
        table = jnp.concatenate([place, moved_len, rank_here[None]]).astype(jnp.int32)
        w_columns, near_queries, near_fresh, near_cache = bring(
            jnp.swapaxes(w_out, 1, 2), queries, new_latent, latent_cache
        )
        table, residual_rows, gain_rows, first_column, w_columns = lax.optimization_barrier(
            (table, residual_rows, gain_rows, first_column, w_columns)
        )
        sent = weigh(
            table, [near_cache] + parts[1:], near_queries, near_fresh, latent_width
        )
        sent_same = gather_equal(sent, "chip", chips)
        head_partial, *expert_weights = project(
            table,
            [near_cache] + parts[1:],
            sent_same,
            swap_core(sent_same),
            w_columns,
            (w_gate[0], w_up[0], w_down[0]),
        )
    else:
        moved = jnp.concatenate(parts).reshape(ranks * slot_count, positions, latent_all)[place]
        position_range = jnp.arange(positions, dtype=jnp.int32)

        def inserted(base, fresh, length):
            for step_index in range(step_count):
                writing = position_range[None, :] == (length + step_index)[:, None]
                base = jnp.where(writing[:, :, None], fresh[:, step_index][:, None, :], base)
            return base

        own_first = rank_here * slot_count
        own_len = lax.dynamic_slice_in_dim(moved_len, own_first, slot_count, 0)
        own_cache = inserted(
            lax.dynamic_slice_in_dim(moved, own_first, slot_count, 0), new_latent, own_len
        )
        visible = (
            position_range[None, None, :]
            < (own_len[:, None] + jnp.arange(step_count, dtype=jnp.int32)[None, :] + 1)[:, :, None]
        )
        scores = (
            jnp.einsum("stha,spa->sthp", queries, own_cache, preferred_element_type=jnp.float32)
            * score_scale
        )
        scores = jnp.where(visible[:, :, None, :], scores, -1e30)
        highest = jnp.max(scores, axis=-1, keepdims=True)
        raised = jnp.exp(scores - highest)
        weights = (raised / jnp.sum(raised, axis=-1, keepdims=True)).astype(jnp.bfloat16)

        weight_count = block_rows * heads_here * positions
        fresh_count = block_rows * latent_width
        lane = 128
        sent = jnp.concatenate(
            [
                weights.reshape(weight_count // lane, lane),
                new_latent[..., :latent_width].reshape(fresh_count // lane, lane),
            ]
        )
        arrived = gather_equal(sent, ("chip", "core"), ranks)
        all_weights = arrived[:, : weight_count // lane].reshape(
            ranks * slot_count, step_count, heads_here, positions
        )
        all_fresh = arrived[:, weight_count // lane :].reshape(
            ranks * slot_count, step_count, latent_width
        )
        all_cache = inserted(moved[..., :latent_width], all_fresh, moved_len)
        attended = jnp.einsum(
            "gthp,gpl->gthl", all_weights, all_cache, preferred_element_type=jnp.float32
        ).astype(jnp.bfloat16)
        head_partial = jnp.dot(
            attended.reshape(row_total, heads_here * latent_width),
            w_out.reshape(heads_here * latent_width, column_count),
            preferred_element_type=jnp.float32,
        ).astype(jnp.bfloat16)
    attn_cols = head_partial.astype(jnp.float32)
    for k in range(1, tp_width):
        attn_cols = attn_cols + swap_tp(head_partial, k).astype(jnp.float32)
    mixed = (residual_rows.astype(jnp.float32) + attn_cols).astype(
        jnp.bfloat16
    )

    same_core = gather_equal(mixed, "chip", chips)
    other_core = swap_core(same_core)
    if with_kernels:
        mine, theirs = run_expert(
            table,
            same_core,
            other_core,
            gain_rows,
            jnp.transpose(experts, (1, 2, 0)),
            jnp.transpose(gate_weights, (1, 2, 0)),
            *expert_weights,
            share,
        )
        leaving = (mine.astype(jnp.float32) + swap_core(theirs).astype(jnp.float32)).astype(
            jnp.bfloat16
        )
    else:
        first = jnp.where(core_here == 0, same_core, other_core)
        second = jnp.where(core_here == 0, other_core, same_core)
        rows_in = jnp.stack([first, second], axis=1).transpose(2, 0, 1, 3).reshape(row_total, -1)
        rows_wide = rows_in.astype(jnp.float32)
        inverse_rms = lax.rsqrt(jnp.mean(rows_wide * rows_wide, axis=-1, keepdims=True) + norm_eps)
        normed = (rows_wide * inverse_rms * norm_gain).astype(jnp.bfloat16)
        gate_proj = jnp.dot(normed, w_gate[0], preferred_element_type=jnp.float32)
        up_proj = jnp.dot(normed, w_up[0], preferred_element_type=jnp.float32)
        activated = (jax.nn.silu(gate_proj) * up_proj).astype(jnp.bfloat16)
        expert_terms = jnp.dot(activated, w_down[0], preferred_element_type=jnp.float32)
        terms = (
            (expert_terms * own_gate)
            .astype(jnp.bfloat16)
            .reshape(row_total, chips, 2, tp_width * share)
            .transpose(2, 1, 0, 3)
        )
        mine = lax.dynamic_index_in_dim(terms, core_here, 0, keepdims=False)
        theirs = lax.dynamic_index_in_dim(terms, 1 - core_here, 0, keepdims=False)
        chip_sum = (mine.astype(jnp.float32) + swap_core(theirs).astype(jnp.float32)).astype(
            jnp.bfloat16
        )
        leaving = (
            chip_sum.reshape(chips, row_total, tp_width, share)
            .transpose(0, 2, 1, 3)
            .reshape(chips * tp_width, row_total, share)
        )
    returned = lax.all_to_all(leaving, ("chip", "tp"), 0, 0, tiled=True)
    moe_part = jnp.sum(returned.astype(jnp.float32), axis=0)
    own_columns = lax.dynamic_slice_in_dim(mixed, first_column, share, 1)
    return (
        (own_columns.astype(jnp.float32) + moe_part)
        .astype(jnp.bfloat16)
        .reshape(residual.shape[0], step_count, share)
    )


def solution(mesh):
    groups, ranks, tp_width = (mesh.shape[name] for name in ("groups", "dp", "tp"))
    split = Mesh(
        mesh.devices.reshape(groups, ranks // 2, 2, tp_width), ("groups", "chip", "core", "tp")
    )
    dp = ("chip", "core")
    placed = (
        P(("groups",) + dp, None, None),
        P("groups"),
        P("groups"),
        P(("groups",) + dp, None, "tp", None),
        P(("groups",) + dp, None, None),
        P("groups", None, dp),
        P("tp", None, dp),
        P(),
        P(dp, None, "tp"),
        P(dp, None, "tp"),
        P(dp, "tp", None),
        P("groups", None, None),
        P("groups", None, None),
    )
    return jax.shard_map(
        body,
        mesh=split,
        in_specs=placed,
        out_specs=P("groups", None, dp + ("tp",)),
        check_vma=False,
    )
```

```python
import jax
import jax.numpy as jnp
from jax import lax
from jax.experimental import pallas as pl
from jax.experimental.pallas import tpu as pltpu
from jax.sharding import Mesh, PartitionSpec as P

score_scale = 192.0 ** (-0.5)
norm_eps = 1e-06


def swap_core(x):
    return lax.ppermute(x, "core", [(0, 1), (1, 0)])


def swap_chip(x, bits):
    count = lax.axis_size("chip")
    return lax.ppermute(x, "chip", [(i, i ^ bits) for i in range(count)])


def swap_tp(x, bits):
    count = lax.axis_size("tp")
    return lax.ppermute(x, "tp", [(i, i ^ bits) for i in range(count)])


def gather_relative(x, near_x, table, wanted):
    chips = lax.axis_size("chip")
    far = [swap_chip(x, 2 * k) for k in range(chips // 2 - 1, 0, -1)][::-1]
    first, table = lax.optimization_barrier((far[0], table))
    far = [first if part is far[0] else part for part in far]
    near = [swap_chip(arrived, 1) for arrived in far[::-1]][::-1]
    if wanted:
        wanted = lax.optimization_barrier((table, *wanted))[1:]
        near[2], *wanted = lax.optimization_barrier((near[2], *bring(*wanted)))
    parts = far[::-1] + [near_x] + near[::-1] + [swap_chip(near_x, 1)]
    return parts + [swap_core(part) for part in parts], table, wanted


def nt_dot(a, b):
    return lax.dot_general(a, b, (((1,), (1,)), ((), ())), preferred_element_type=jnp.float32)


def inserted_rows(base, fresh, length):
    position = lax.broadcasted_iota(jnp.int32, base.shape, 0)
    for step_index, row in enumerate(fresh):
        base = jnp.where(position == length + step_index, row, base)
    return base


def bring_kernel(*refs):
    count = len(refs) // 2
    copies = [
        pltpu.make_async_copy(refs[k], refs[count + k], refs[-1].at[k]) for k in range(count)
    ]
    for copy in copies:
        copy.start()
    for copy in copies:
        copy.wait()


def weigh_kernel(table, *refs):
    parts, (queries, new_latent, out) = refs[:-3], refs[-3:]
    slot_count, positions, _ = parts[0].shape
    step_count, heads, _ = queries.shape[1:]
    width = out.shape[1]
    requests = len(parts) * slot_count
    rank = table[table.shape[0] - 2]
    slabs = []
    for s in range(slot_count):
        length = table[requests + rank * slot_count + s]
        place = table[rank * slot_count + s]
        held = parts[0][s]
        for k in range(1, len(parts)):
            held = jnp.where(place == k * slot_count + s, parts[k][s], held)
        fresh = [new_latent[s, t : t + 1, :].astype(jnp.float32) for t in range(step_count)]
        keys = inserted_rows(held.astype(jnp.float32), fresh, length).astype(jnp.bfloat16)
        rows = queries[s].reshape(step_count * heads, keys.shape[1])
        scores = nt_dot(rows, keys) * score_scale
        step_of = lax.broadcasted_iota(jnp.int32, scores.shape, 0) // heads
        position = lax.broadcasted_iota(jnp.int32, scores.shape, 1)
        scores = jnp.where(position < length + step_of + 1, scores, -1e30)
        raised = jnp.exp(scores - jnp.max(scores, axis=-1, keepdims=True))
        weights = raised / jnp.sum(raised, axis=-1, keepdims=True)
        slabs += [weights[k * 8 : (k + 1) * 8] for k in range(step_count * heads // 8)]
    top = jnp.concatenate(slabs, axis=1)
    row = lax.broadcasted_iota(jnp.int32, (8, width), 0)
    bottom = jnp.zeros((8, width), jnp.float32)
    for s in range(slot_count):
        for t in range(step_count):
            bottom = jnp.where(
                row == s * step_count + t,
                new_latent[s, t : t + 1, :width].astype(jnp.float32),
                bottom,
            )
    out[...] = jnp.concatenate([top, bottom], axis=0).astype(out.dtype)


def project_kernel(table, *refs):
    later = refs[-1].shape[0]
    cut = len(refs) - 11 - 2 * later
    parts, rest = refs[:cut], refs[cut:]
    sent_same, sent_other, residual, w_out = rest[:4]
    sources, (out, residual_rows), targets = rest[4 : 4 + later], rest[4 + later : 6 + later], rest[6 + later : 6 + 2 * later]
    wide, fresh, keys, attended, load_sems = rest[6 + 2 * later :]
    slot_count, positions, _ = parts[0].shape
    requests = len(parts) * slot_count
    heads, columns, latent_width = w_out.shape
    chips = sent_same.shape[0]
    step_count = 2
    loads = [
        pltpu.make_async_copy(source, target, load_sems.at[k])
        for k, (source, target) in enumerate(zip(sources, targets))
    ]
    for load in loads:
        load.start()
    core = table[table.shape[0] - 2] % 2
    lanes = 128
    for k, ref in enumerate((sent_same, sent_other)):
        for c in range(chips):
            for g in range(slot_count * step_count):
                wide[k, g, c * 8 : (c + 1) * 8, :] = ref[
                    c, :8, g * lanes : (g + 1) * lanes
                ].astype(jnp.float32)
            fresh[k, c] = ref[c, 8:, :].astype(jnp.float32)
    per_lane = lanes // positions
    group_rows = 8 * step_count * chips
    row = lax.broadcasted_iota(jnp.int32, (group_rows, lanes), 0) % chips
    lane = lax.broadcasted_iota(jnp.int32, (group_rows, lanes), 1) // positions
    own_block = [row == lane + first for first in range(0, chips, per_lane)]
    taken = step_count * chips
    spaced = []
    for s in range(slot_count):
        for k in range(2):
            rows = [
                wide[k, s * step_count + t, pl.ds(q, chips, stride=8), :]
                for q in range(8)
                for t in range(step_count)
            ]
            packed = jnp.concatenate(rows, axis=0)
            turned = []
            for r in range(per_lane):
                x = jnp.where(lane == r, packed, 0.0)
                shift = positions
                while shift < lanes:
                    x = x + pltpu.roll(x, shift, 1)
                    shift *= 2
                turned.append(x)
            spaced.append(
                jnp.concatenate(
                    [
                        jnp.concatenate([jnp.where(m, x, 0.0) for m in own_block], axis=1)
                        for x in turned
                    ],
                    axis=0,
                ).astype(jnp.bfloat16)
            )
    for n, part in enumerate(parts):
        for s in range(slot_count):
            request = table[2 * requests + n * slot_count + s]
            length = table[requests + request]
            owner = request // slot_count
            c = owner // 2
            k = (owner % 2) ^ core
            rows = [
                fresh[k, c, s * step_count + t : s * step_count + t + 1, :]
                for t in range(step_count)
            ]
            first = pl.multiple_of(c * positions, positions)
            keys[s * 2 + k, pl.ds(first, positions), :] = inserted_rows(
                part[s, :, :latent_width].astype(jnp.float32), rows, length
            ).astype(jnp.bfloat16)
    for s in range(slot_count):
        for k in range(2):
            group = s * 2 + k
            product = jnp.dot(
                spaced[group], keys[group], preferred_element_type=jnp.float32
            ).astype(jnp.bfloat16)
            for h in range(heads):
                attended[h, group * taken : (group + 1) * taken, :] = product[
                    h * taken : (h + 1) * taken
                ]
    total = jnp.zeros((attended.shape[1], columns), jnp.float32)
    for h in range(heads):
        total = total + nt_dot(attended[h], w_out[h])
    count = total.shape[0]
    to = lax.broadcasted_iota(jnp.int32, (count, count), 0)
    source = lax.broadcasted_iota(jnp.int32, (count, count), 1)
    core_of, slot_of, step_of = (to // 4) % 2, (to // 2) % 2, to % 2
    relative = jnp.where(core == 0, core_of, 1 - core_of)
    moved = (slot_of * 2 + relative) * taken + step_of * chips + to // 8
    order = (source == moved).astype(jnp.bfloat16)
    out[...] = jnp.dot(
        order, total.astype(jnp.bfloat16), preferred_element_type=jnp.float32
    ).astype(out.dtype)
    row = lax.broadcasted_iota(jnp.int32, (count, count // step_count), 0)
    column = lax.broadcasted_iota(jnp.int32, (count, count // step_count), 1)
    straight = jnp.zeros((count, columns), jnp.float32)
    for t in range(step_count):
        here = (row == column * step_count + t).astype(jnp.bfloat16)
        straight += jnp.dot(here, residual[:, t, :], preferred_element_type=jnp.float32)
    residual_rows[...] = straight.astype(residual_rows.dtype)
    for load in loads:
        load.wait()


def expert_kernel(
    table, same, other, gain, experts, gates, w_gate, w_up, w_down, keep, give, own, normed
):
    chips, rows, columns = same.shape
    features = chips * 2 * columns
    rank = table[table.shape[0] - 2]
    core = rank % 2
    squares = jnp.zeros((rows, columns), jnp.float32)
    for ref in (same, other):
        for c in range(chips):
            x = ref[c].astype(jnp.float32)
            squares = squares + x * x
    scale = lax.rsqrt(jnp.sum(squares, axis=1, keepdims=True) / features + norm_eps)
    for first in range(0, chips, 2):
        pieces = []
        for c in range(first, first + 2):
            a, b = same[c].astype(jnp.float32), other[c].astype(jnp.float32)
            pieces.append(jnp.where(core == 0, a, b))
            pieces.append(jnp.where(core == 0, b, a))
        width = 4 * columns
        start = first * 2 * columns
        gains = [gain[k : k + 1, :] for k in range(start // 128, (start + width) // 128)]
        normed[:, start : start + width] = (
            jnp.concatenate(pieces, axis=1) * scale * jnp.concatenate(gains, axis=1)
        ).astype(normed.dtype)
    gate_proj = jnp.dot(normed[...], w_gate[...], preferred_element_type=jnp.float32)
    up_proj = jnp.dot(normed[...], w_up[...], preferred_element_type=jnp.float32)
    by_step = jnp.sum(jnp.where(experts[...] == rank, gates[...], 0.0), axis=1)
    steps, requests = by_step.shape
    row = lax.broadcasted_iota(jnp.int32, (rows, requests), 0)
    request = lax.broadcasted_iota(jnp.int32, (rows, requests), 1)
    own_gate = jnp.zeros((rows, 1), jnp.float32)
    for t in range(steps):
        here = request * steps + t == row
        own_gate += jnp.sum(jnp.where(here, by_step[t : t + 1], 0.0), axis=1, keepdims=True)
    activated = (gate_proj / (1.0 + jnp.exp(-gate_proj)) * up_proj * own_gate).astype(
        jnp.bfloat16
    )
    share = keep.shape[2]
    mixed = same[rank // 2].astype(jnp.float32)
    tp = table[table.shape[0] - 1]
    own[...] = jnp.where(tp == 0, mixed[:, :share], mixed[:, share:]).astype(own.dtype)
    tile = 8 * share
    for first in range(0, features, tile):
        terms = jnp.dot(
            activated, w_down[:, first : first + tile], preferred_element_type=jnp.float32
        ).astype(keep.dtype)
        pieces = [terms[:, j * share : (j + 1) * share] for j in range(8)]

        def put(even, odd):
            for j in range(8):
                target = even if (j // 2) % 2 == 0 else odd
                target[(first // tile) * 4 + (j // 4) * 2 + j % 2] = pieces[j]

        @pl.when(core == 0)
        def _():
            put(keep, give)

        @pl.when(core == 1)
        def _():
            put(give, keep)


VMEM = pl.BlockSpec(memory_space=pltpu.VMEM)
SMEM = pl.BlockSpec(memory_space=pltpu.SMEM)
ANY = pl.BlockSpec(memory_space=pl.ANY)


def in_vmem(x):
    return pltpu.with_memory_space_constraint(x, pltpu.VMEM)


def in_hbm(x):
    return pltpu.with_memory_space_constraint(x, pltpu.HBM)


def bring(*arrays):
    return pl.pallas_call(
        bring_kernel,
        out_shape=[pltpu.VMEM(x.shape, x.dtype) for x in arrays],
        in_specs=[ANY] * len(arrays),
        out_specs=[VMEM] * len(arrays),
        scratch_shapes=[pltpu.SemaphoreType.DMA((len(arrays),))],
        compiler_params=pltpu.CompilerParams(vmem_limit_bytes=2 * 2**20),
        cost_estimate=pl.CostEstimate(
            flops=0, bytes_accessed=sum(4 * x.size for x in arrays), transcendentals=0
        ),
        name="bring_to_vmem",
    )(*[in_hbm(x) for x in arrays])


def weigh(table, parts, queries, new_latent, latent_width):
    return pl.pallas_call(
        weigh_kernel,
        out_shape=jax.ShapeDtypeStruct((16, latent_width), jnp.bfloat16),
        in_specs=[SMEM] + [VMEM] * (len(parts) + 2),
        out_specs=VMEM,
        compiler_params=pltpu.CompilerParams(vmem_limit_bytes=8 * 2**20),
        name="softmax_weights",
    )(table, *[in_vmem(x) for x in (*parts, queries, new_latent)])


def project(table, parts, sent_same, sent_other, residual, w_out, later):
    heads, columns, latent_width = w_out.shape
    slot_count, positions, _ = parts[0].shape
    chips = sent_same.shape[0]
    rows = residual.shape[0] * residual.shape[1]
    small = jax.ShapeDtypeStruct((rows, columns), jnp.bfloat16)
    return pl.pallas_call(
        project_kernel,
        out_shape=[small, small] + [pltpu.VMEM(x.shape, x.dtype) for x in later],
        in_specs=[SMEM] + [VMEM] * (len(parts) + 4) + [ANY] * len(later),
        out_specs=[VMEM] * (2 + len(later)),
        scratch_shapes=[
            pltpu.VMEM((2, 4, chips * 8, 128), jnp.float32),
            pltpu.VMEM((2, chips, 8, latent_width), jnp.float32),
            pltpu.VMEM((4, chips * positions, latent_width), jnp.bfloat16),
            pltpu.VMEM((heads, rows, latent_width), jnp.bfloat16),
            pltpu.SemaphoreType.DMA((len(later),)),
        ],
        compiler_params=pltpu.CompilerParams(vmem_limit_bytes=8 * 2**20),
        cost_estimate=pl.CostEstimate(
            flops=0, bytes_accessed=60 * 2**20, transcendentals=0
        ),
        name="attend_project",
    )(
        table,
        *[in_vmem(part) for part in parts],
        sent_same,
        sent_other,
        in_vmem(residual),
        in_vmem(w_out),
        *[in_hbm(x) for x in later],
    )


def run_expert(table, same, other, gain, experts, gates, w_gate, w_up, w_down, share):
    chips, rows, _ = same.shape
    shape = jax.ShapeDtypeStruct((chips * 2, rows, share), jnp.bfloat16)
    return pl.pallas_call(
        expert_kernel,
        out_shape=(shape, shape, jax.ShapeDtypeStruct((rows, share), jnp.bfloat16)),
        in_specs=[SMEM] + [VMEM] * 8,
        out_specs=(VMEM, VMEM, VMEM),
        scratch_shapes=[
            pltpu.VMEM((rows, gain.size), jnp.bfloat16),
        ],
        compiler_params=pltpu.CompilerParams(vmem_limit_bytes=8 * 2**20),
        name="expert_mlp",
    )(
        table,
        same,
        other,
        gain,
        experts,
        gates,
        in_vmem(w_gate),
        in_vmem(w_up),
        in_vmem(w_down),
    )


def gather_equal(x, axes, count):
    spread = jnp.broadcast_to(x[None], (count,) + x.shape)
    return lax.all_to_all(spread, axes, 0, 0, tiled=True)


def body(
    latent_cache,
    lengths,
    destination,
    queries,
    new_latent,
    residual,
    w_out,
    norm_gain,
    w_gate,
    w_up,
    w_down,
    experts,
    gate_weights,
):
    chips = lax.axis_size("chip")
    tp_width = lax.axis_size("tp")
    ranks = chips * 2
    chip_here = lax.axis_index("chip")
    core_here = lax.axis_index("core")
    tp_here = lax.axis_index("tp")
    rank_here = chip_here * 2 + core_here
    slot_count, positions, latent_all = latent_cache.shape
    heads_here, latent_width, column_count = w_out.shape
    step_count = queries.shape[1]
    block_rows = slot_count * step_count
    row_total = ranks * block_rows

    slots = jnp.tile(jnp.arange(slot_count, dtype=jnp.int32), ranks)
    request = jnp.arange(ranks * slot_count, dtype=jnp.int32)
    goes_to = destination * slot_count + slots
    source = jnp.sum(
        jnp.where(goes_to[None, :] == request[:, None], request[None, :], 0), axis=1
    )
    moved_len = jnp.sum(
        jnp.where(goes_to[None, :] == request[:, None], lengths[None, :], 0), axis=1
    )
    relative = (source // slot_count) ^ rank_here
    place = (
        (
            (relative & 1) * chips
            + ((relative >> 1) & 1) * (chips // 2)
            + (chips // 2 - 1 - (relative >> 2))
        )
        * slot_count
        + source % slot_count
    )
    served = jnp.sum(
        jnp.where(place[None, :] == request[:, None], request[None, :], 0), axis=1
    )
    table = jnp.concatenate(
        [place, moved_len, served, rank_here[None], tp_here[None]]
    ).astype(jnp.int32)
    with_kernels = (
        slot_count == 2
        and step_count == 2
        and chips == 8
        and tp_width == 2
        and (positions, heads_here, latent_width, column_count) == (32, 32, 512, 224)
    )
    near_cache = latent_cache
    if with_kernels:
        near_cache, near_queries, near_fresh = bring(latent_cache, queries, new_latent)
    wanted = [jnp.swapaxes(w_out, 1, 2), residual] if with_kernels else []
    parts, table, wanted = gather_relative(latent_cache, near_cache, table, wanted)
    own_gate = jnp.sum(jnp.where(experts == rank_here, gate_weights, 0.0), axis=2).reshape(
        row_total, 1
    )
    share = column_count // tp_width
    if with_kernels:
        w_columns, near_residual = wanted
        sent = weigh(table, parts, near_queries, near_fresh, latent_width)
        sent_same = gather_equal(sent, "chip", chips)
        head_partial, residual_rows, *expert_weights = project(
            table,
            parts,
            sent_same,
            swap_core(sent_same),
            near_residual,
            w_columns,
            (w_down[0],),
        )
    else:
        moved = jnp.concatenate(parts).reshape(ranks * slot_count, positions, latent_all)[place]
        position_range = jnp.arange(positions, dtype=jnp.int32)

        def inserted(base, fresh, length):
            for step_index in range(step_count):
                writing = position_range[None, :] == (length + step_index)[:, None]
                base = jnp.where(writing[:, :, None], fresh[:, step_index][:, None, :], base)
            return base

        own_first = rank_here * slot_count
        own_len = lax.dynamic_slice_in_dim(moved_len, own_first, slot_count, 0)
        own_cache = inserted(
            lax.dynamic_slice_in_dim(moved, own_first, slot_count, 0), new_latent, own_len
        )
        visible = (
            position_range[None, None, :]
            < (own_len[:, None] + jnp.arange(step_count, dtype=jnp.int32)[None, :] + 1)[:, :, None]
        )
        scores = (
            jnp.einsum("stha,spa->sthp", queries, own_cache, preferred_element_type=jnp.float32)
            * score_scale
        )
        scores = jnp.where(visible[:, :, None, :], scores, -1e30)
        highest = jnp.max(scores, axis=-1, keepdims=True)
        raised = jnp.exp(scores - highest)
        weights = (raised / jnp.sum(raised, axis=-1, keepdims=True)).astype(jnp.bfloat16)

        weight_count = block_rows * heads_here * positions
        fresh_count = block_rows * latent_width
        lane = 128
        sent = jnp.concatenate(
            [
                weights.reshape(weight_count // lane, lane),
                new_latent[..., :latent_width].reshape(fresh_count // lane, lane),
            ]
        )
        arrived = gather_equal(sent, ("chip", "core"), ranks)
        all_weights = arrived[:, : weight_count // lane].reshape(
            ranks * slot_count, step_count, heads_here, positions
        )
        all_fresh = arrived[:, weight_count // lane :].reshape(
            ranks * slot_count, step_count, latent_width
        )
        all_cache = inserted(moved[..., :latent_width], all_fresh, moved_len)
        attended = jnp.einsum(
            "gthp,gpl->gthl", all_weights, all_cache, preferred_element_type=jnp.float32
        ).astype(jnp.bfloat16)
        head_partial = jnp.dot(
            attended.reshape(row_total, heads_here * latent_width),
            w_out.reshape(heads_here * latent_width, column_count),
            preferred_element_type=jnp.float32,
        ).astype(jnp.bfloat16)
    if not with_kernels:
        residual_rows = residual.reshape(row_total, column_count)
    attn_cols = head_partial.astype(jnp.float32)
    for k in range(1, tp_width):
        attn_cols = attn_cols + swap_tp(head_partial, k).astype(jnp.float32)
    mixed = (residual_rows.astype(jnp.float32) + attn_cols).astype(
        jnp.bfloat16
    )

    same_core = gather_equal(mixed, "chip", chips)
    other_core = swap_core(same_core)
    if with_kernels:
        mine, theirs, own_columns = run_expert(
            table,
            same_core,
            other_core,
            norm_gain.reshape(norm_gain.size // 128, 128),
            jnp.transpose(experts, (1, 2, 0)),
            jnp.transpose(gate_weights, (1, 2, 0)),
            w_gate[0],
            w_up[0],
            *expert_weights,
            share,
        )
        leaving = (mine.astype(jnp.float32) + swap_core(theirs).astype(jnp.float32)).astype(
            jnp.bfloat16
        )
    else:
        first = jnp.where(core_here == 0, same_core, other_core)
        second = jnp.where(core_here == 0, other_core, same_core)
        rows_in = jnp.stack([first, second], axis=1).transpose(2, 0, 1, 3).reshape(row_total, -1)
        rows_wide = rows_in.astype(jnp.float32)
        inverse_rms = lax.rsqrt(jnp.mean(rows_wide * rows_wide, axis=-1, keepdims=True) + norm_eps)
        normed = (rows_wide * inverse_rms * norm_gain).astype(jnp.bfloat16)
        gate_proj = jnp.dot(normed, w_gate[0], preferred_element_type=jnp.float32)
        up_proj = jnp.dot(normed, w_up[0], preferred_element_type=jnp.float32)
        activated = (jax.nn.silu(gate_proj) * up_proj).astype(jnp.bfloat16)
        expert_terms = jnp.dot(activated, w_down[0], preferred_element_type=jnp.float32)
        terms = (
            (expert_terms * own_gate)
            .astype(jnp.bfloat16)
            .reshape(row_total, chips, 2, tp_width * share)
            .transpose(2, 1, 0, 3)
        )
        mine = lax.dynamic_index_in_dim(terms, core_here, 0, keepdims=False)
        theirs = lax.dynamic_index_in_dim(terms, 1 - core_here, 0, keepdims=False)
        chip_sum = (mine.astype(jnp.float32) + swap_core(theirs).astype(jnp.float32)).astype(
            jnp.bfloat16
        )
        leaving = (
            chip_sum.reshape(chips, row_total, tp_width, share)
            .transpose(0, 2, 1, 3)
            .reshape(chips * tp_width, row_total, share)
        )
    returned = lax.all_to_all(leaving, ("chip", "tp"), 0, 0, tiled=True)
    moe_part = jnp.sum(returned.astype(jnp.float32), axis=0)
    if not with_kernels:
        own_columns = lax.dynamic_slice_in_dim(mixed, tp_here * share, share, 1)
    return (
        (own_columns.astype(jnp.float32) + moe_part)
        .astype(jnp.bfloat16)
        .reshape(residual.shape[0], step_count, share)
    )


def solution(mesh):
    groups, ranks, tp_width = (mesh.shape[name] for name in ("groups", "dp", "tp"))
    split = Mesh(
        mesh.devices.reshape(groups, ranks // 2, 2, tp_width), ("groups", "chip", "core", "tp")
    )
    dp = ("chip", "core")
    placed = (
        P(("groups",) + dp, None, None),
        P("groups"),
        P("groups"),
        P(("groups",) + dp, None, "tp", None),
        P(("groups",) + dp, None, None),
        P("groups", None, dp),
        P("tp", None, dp),
        P(),
        P(dp, None, "tp"),
        P(dp, None, "tp"),
        P(dp, "tp", None),
        P("groups", None, None),
        P("groups", None, None),
    )
    return jax.shard_map(
        body,
        mesh=split,
        in_specs=placed,
        out_specs=P("groups", None, dp + ("tp",)),
        check_vma=False,
    )
```

```python
import jax
import jax.numpy as jnp
from jax import lax
from jax.experimental import pallas as pl
from jax.experimental.pallas import tpu as pltpu
from jax.sharding import Mesh, PartitionSpec as P

score_scale = 192.0 ** (-0.5)
norm_eps = 1e-06


def swap_core(x):
    return lax.ppermute(x, "core", [(0, 1), (1, 0)])


def swap_chip(x, bits):
    count = lax.axis_size("chip")
    return lax.ppermute(x, "chip", [(i, i ^ bits) for i in range(count)])


def swap_tp(x, bits):
    count = lax.axis_size("tp")
    return lax.ppermute(x, "tp", [(i, i ^ bits) for i in range(count)])


def gather_relative(x, near_x, table, wanted):
    chips = lax.axis_size("chip")
    far = [swap_chip(x, 2 * k) for k in range(chips // 2 - 1, 0, -1)][::-1]
    first, table = lax.optimization_barrier((far[0], table))
    far = [first if part is far[0] else part for part in far]
    near = [swap_chip(arrived, 1) for arrived in far[::-1]][::-1]
    if wanted:
        wanted = lax.optimization_barrier((table, *wanted))[1:]
        near[2], *wanted = lax.optimization_barrier((near[2], *bring(*wanted)))
    parts = far[::-1] + [near_x] + near[::-1] + [swap_chip(near_x, 1)]
    return parts + [swap_core(part) for part in parts], table, wanted


def nt_dot(a, b):
    return lax.dot_general(a, b, (((1,), (1,)), ((), ())), preferred_element_type=jnp.float32)


def inserted_rows(base, fresh, length):
    position = lax.broadcasted_iota(jnp.int32, base.shape, 0)
    for step_index, row in enumerate(fresh):
        base = jnp.where(position == length + step_index, row, base)
    return base


def bring_kernel(*refs):
    count = len(refs) // 2
    copies = [
        pltpu.make_async_copy(refs[k], refs[count + k], refs[-1].at[k]) for k in range(count)
    ]
    for copy in copies:
        copy.start()
    for copy in copies:
        copy.wait()


def weigh_kernel(table, *refs):
    parts, (queries, new_latent, out) = refs[:-3], refs[-3:]
    slot_count, positions, _ = parts[0].shape
    step_count, heads, _ = queries.shape[1:]
    width = out.shape[1]
    requests = len(parts) * slot_count
    rank = table[table.shape[0] - 2]
    slabs = []
    for s in range(slot_count):
        length = table[requests + rank * slot_count + s]
        place = table[rank * slot_count + s]
        held = parts[0][s]
        for k in range(1, len(parts)):
            held = jnp.where(place == k * slot_count + s, parts[k][s], held)
        fresh = [new_latent[s, t : t + 1, :].astype(jnp.float32) for t in range(step_count)]
        keys = inserted_rows(held.astype(jnp.float32), fresh, length).astype(jnp.bfloat16)
        rows = queries[s].reshape(step_count * heads, keys.shape[1])
        scores = nt_dot(rows, keys) * score_scale
        step_of = lax.broadcasted_iota(jnp.int32, scores.shape, 0) // heads
        position = lax.broadcasted_iota(jnp.int32, scores.shape, 1)
        scores = jnp.where(position < length + step_of + 1, scores, -1e30)
        raised = jnp.exp(scores - jnp.max(scores, axis=-1, keepdims=True))
        weights = raised / jnp.sum(raised, axis=-1, keepdims=True)
        slabs += [weights[k * 8 : (k + 1) * 8] for k in range(step_count * heads // 8)]
    top = jnp.concatenate(slabs, axis=1)
    row = lax.broadcasted_iota(jnp.int32, (8, width), 0)
    bottom = jnp.zeros((8, width), jnp.float32)
    for s in range(slot_count):
        for t in range(step_count):
            bottom = jnp.where(
                row == s * step_count + t,
                new_latent[s, t : t + 1, :width].astype(jnp.float32),
                bottom,
            )
    out[...] = jnp.concatenate([top, bottom], axis=0).astype(out.dtype)


def project_kernel(table, *refs):
    later = refs[-1].shape[0]
    cut = len(refs) - 11 - 2 * later
    parts, rest = refs[:cut], refs[cut:]
    sent_same, sent_other, residual, w_out = rest[:4]
    sources, (out, residual_rows), targets = rest[4 : 4 + later], rest[4 + later : 6 + later], rest[6 + later : 6 + 2 * later]
    wide, fresh, keys, attended, load_sems = rest[6 + 2 * later :]
    slot_count, positions, _ = parts[0].shape
    requests = len(parts) * slot_count
    heads, columns, latent_width = w_out.shape
    chips = sent_same.shape[0]
    step_count = 2
    loads = [
        pltpu.make_async_copy(source, target, load_sems.at[k])
        for k, (source, target) in enumerate(zip(sources, targets))
    ]
    for load in loads:
        load.start()
    core = table[table.shape[0] - 2] % 2
    lanes = 128
    for k, ref in enumerate((sent_same, sent_other)):
        for c in range(chips):
            chunk = ref[c].astype(jnp.float32)
            for g in range(slot_count * step_count):
                wide[k, g, c * 8 : (c + 1) * 8, :] = chunk[:8, g * lanes : (g + 1) * lanes]
            fresh[k, c] = chunk[8:]
    per_lane = lanes // positions
    group_rows = 8 * step_count * chips
    row = lax.broadcasted_iota(jnp.int32, (group_rows, lanes), 0) % chips
    lane = lax.broadcasted_iota(jnp.int32, (group_rows, lanes), 1) // positions
    own_block = [row == lane + first for first in range(0, chips, per_lane)]
    taken = step_count * chips
    spaced = []
    for s in range(slot_count):
        for k in range(2):
            rows = [
                wide[k, s * step_count + t, pl.ds(q, chips, stride=8), :]
                for q in range(8)
                for t in range(step_count)
            ]
            packed = jnp.concatenate(rows, axis=0)
            turned = []
            for r in range(per_lane):
                x = jnp.where(lane == r, packed, 0.0)
                shift = positions
                while shift < lanes:
                    x = x + pltpu.roll(x, shift, 1)
                    shift *= 2
                turned.append(x)
            spaced.append(
                jnp.concatenate(
                    [
                        jnp.concatenate([jnp.where(m, x, 0.0) for m in own_block], axis=1)
                        for x in turned
                    ],
                    axis=0,
                ).astype(jnp.bfloat16)
            )
    for n, part in enumerate(parts):
        for s in range(slot_count):
            request = table[2 * requests + n * slot_count + s]
            length = table[requests + request]
            owner = request // slot_count
            c = owner // 2
            k = (owner % 2) ^ core
            rows = [
                fresh[k, c, s * step_count + t : s * step_count + t + 1, :]
                for t in range(step_count)
            ]
            first = pl.multiple_of(c * positions, positions)
            keys[s * 2 + k, pl.ds(first, positions), :] = inserted_rows(
                part[s, :, :latent_width].astype(jnp.float32), rows, length
            ).astype(jnp.bfloat16)
    for s in range(slot_count):
        for k in range(2):
            group = s * 2 + k
            product = jnp.dot(
                spaced[group], keys[group], preferred_element_type=jnp.float32
            ).astype(jnp.bfloat16)
            for h in range(heads):
                attended[h, group * taken : (group + 1) * taken, :] = product[
                    h * taken : (h + 1) * taken
                ]
    total = jnp.zeros((attended.shape[1], columns), jnp.float32)
    for h in range(heads):
        total = total + nt_dot(attended[h], w_out[h])
    count = total.shape[0]
    to = lax.broadcasted_iota(jnp.int32, (count, count), 0)
    source = lax.broadcasted_iota(jnp.int32, (count, count), 1)
    core_of, slot_of, step_of = (to // 4) % 2, (to // 2) % 2, to % 2
    relative = jnp.where(core == 0, core_of, 1 - core_of)
    moved = (slot_of * 2 + relative) * taken + step_of * chips + to // 8
    order = (source == moved).astype(jnp.bfloat16)
    out[...] = jnp.dot(
        order, total.astype(jnp.bfloat16), preferred_element_type=jnp.float32
    ).astype(out.dtype)
    row = lax.broadcasted_iota(jnp.int32, (count, count // step_count), 0)
    column = lax.broadcasted_iota(jnp.int32, (count, count // step_count), 1)
    straight = jnp.zeros((count, columns), jnp.float32)
    wide_residual = residual[...].astype(jnp.float32)
    for t in range(step_count):
        here = (row == column * step_count + t).astype(jnp.bfloat16)
        rows = wide_residual[:, t, :].astype(jnp.bfloat16)
        straight += jnp.dot(here, rows, preferred_element_type=jnp.float32)
    residual_rows[...] = straight.astype(residual_rows.dtype)
    for load in loads:
        load.wait()


def expert_kernel(
    table, same, other, gain, experts, gates, w_gate, w_up, w_down, keep, give, own, normed
):
    chips, rows, columns = same.shape
    features = chips * 2 * columns
    rank = table[table.shape[0] - 2]
    core = rank % 2
    squares = jnp.zeros((rows, columns), jnp.float32)
    for ref in (same, other):
        for c in range(chips):
            x = ref[c].astype(jnp.float32)
            squares = squares + x * x
    scale = lax.rsqrt(jnp.sum(squares, axis=1, keepdims=True) / features + norm_eps)
    for first in range(0, chips, 2):
        pieces = []
        for c in range(first, first + 2):
            a, b = same[c].astype(jnp.float32), other[c].astype(jnp.float32)
            pieces.append(jnp.where(core == 0, a, b))
            pieces.append(jnp.where(core == 0, b, a))
        width = 4 * columns
        start = first * 2 * columns
        gains = [gain[k : k + 1, :] for k in range(start // 128, (start + width) // 128)]
        normed[:, start : start + width] = (
            jnp.concatenate(pieces, axis=1) * scale * jnp.concatenate(gains, axis=1)
        ).astype(normed.dtype)
    gate_proj = jnp.dot(normed[...], w_gate[...], preferred_element_type=jnp.float32)
    up_proj = jnp.dot(normed[...], w_up[...], preferred_element_type=jnp.float32)
    by_step = jnp.sum(jnp.where(experts[...] == rank, gates[...], 0.0), axis=1)
    steps, requests = by_step.shape
    row = lax.broadcasted_iota(jnp.int32, (rows, requests), 0)
    request = lax.broadcasted_iota(jnp.int32, (rows, requests), 1)
    own_gate = jnp.zeros((rows, 1), jnp.float32)
    for t in range(steps):
        here = request * steps + t == row
        own_gate += jnp.sum(jnp.where(here, by_step[t : t + 1], 0.0), axis=1, keepdims=True)
    activated = (gate_proj / (1.0 + jnp.exp(-gate_proj)) * up_proj * own_gate).astype(
        jnp.bfloat16
    )
    share = keep.shape[2]
    mixed = same[rank // 2].astype(jnp.float32)
    tp = table[table.shape[0] - 1]
    own[...] = jnp.where(tp == 0, mixed[:, :share], mixed[:, share:]).astype(own.dtype)
    tile = 8 * share
    for first in range(0, features, tile):
        terms = jnp.dot(
            activated, w_down[:, first : first + tile], preferred_element_type=jnp.float32
        ).astype(keep.dtype)
        pieces = [terms[:, j * share : (j + 1) * share] for j in range(8)]

        def put(even, odd):
            for j in range(8):
                target = even if (j // 2) % 2 == 0 else odd
                target[(first // tile) * 4 + (j // 4) * 2 + j % 2] = pieces[j]

        @pl.when(core == 0)
        def _():
            put(keep, give)

        @pl.when(core == 1)
        def _():
            put(give, keep)


VMEM = pl.BlockSpec(memory_space=pltpu.VMEM)
SMEM = pl.BlockSpec(memory_space=pltpu.SMEM)
ANY = pl.BlockSpec(memory_space=pl.ANY)


def in_vmem(x):
    return pltpu.with_memory_space_constraint(x, pltpu.VMEM)


def in_hbm(x):
    return pltpu.with_memory_space_constraint(x, pltpu.HBM)


def bring(*arrays):
    return pl.pallas_call(
        bring_kernel,
        out_shape=[pltpu.VMEM(x.shape, x.dtype) for x in arrays],
        in_specs=[ANY] * len(arrays),
        out_specs=[VMEM] * len(arrays),
        scratch_shapes=[pltpu.SemaphoreType.DMA((len(arrays),))],
        compiler_params=pltpu.CompilerParams(vmem_limit_bytes=2 * 2**20),
        cost_estimate=pl.CostEstimate(
            flops=0, bytes_accessed=sum(4 * x.size for x in arrays), transcendentals=0
        ),
        name="bring_to_vmem",
    )(*[in_hbm(x) for x in arrays])


def weigh(table, parts, queries, new_latent, latent_width):
    return pl.pallas_call(
        weigh_kernel,
        out_shape=jax.ShapeDtypeStruct((16, latent_width), jnp.bfloat16),
        in_specs=[SMEM] + [VMEM] * (len(parts) + 2),
        out_specs=VMEM,
        compiler_params=pltpu.CompilerParams(vmem_limit_bytes=8 * 2**20),
        name="softmax_weights",
    )(table, *[in_vmem(x) for x in (*parts, queries, new_latent)])


def project(table, parts, sent_same, sent_other, residual, w_out, later):
    heads, columns, latent_width = w_out.shape
    slot_count, positions, _ = parts[0].shape
    chips = sent_same.shape[0]
    rows = residual.shape[0] * residual.shape[1]
    small = jax.ShapeDtypeStruct((rows, columns), jnp.bfloat16)
    return pl.pallas_call(
        project_kernel,
        out_shape=[small, small] + [pltpu.VMEM(x.shape, x.dtype) for x in later],
        in_specs=[SMEM] + [VMEM] * (len(parts) + 4) + [ANY] * len(later),
        out_specs=[VMEM] * (2 + len(later)),
        scratch_shapes=[
            pltpu.VMEM((2, 4, chips * 8, 128), jnp.float32),
            pltpu.VMEM((2, chips, 8, latent_width), jnp.float32),
            pltpu.VMEM((4, chips * positions, latent_width), jnp.bfloat16),
            pltpu.VMEM((heads, rows, latent_width), jnp.bfloat16),
            pltpu.SemaphoreType.DMA((len(later),)),
        ],
        compiler_params=pltpu.CompilerParams(vmem_limit_bytes=8 * 2**20),
        cost_estimate=pl.CostEstimate(
            flops=0, bytes_accessed=60 * 2**20, transcendentals=0
        ),
        name="attend_project",
    )(
        table,
        *[in_vmem(part) for part in parts],
        sent_same,
        sent_other,
        in_vmem(residual),
        in_vmem(w_out),
        *[in_hbm(x) for x in later],
    )


def run_expert(table, same, other, gain, experts, gates, w_gate, w_up, w_down, share):
    chips, rows, _ = same.shape
    shape = jax.ShapeDtypeStruct((chips * 2, rows, share), jnp.bfloat16)
    return pl.pallas_call(
        expert_kernel,
        out_shape=(shape, shape, jax.ShapeDtypeStruct((rows, share), jnp.bfloat16)),
        in_specs=[SMEM] + [VMEM] * 8,
        out_specs=(VMEM, VMEM, VMEM),
        scratch_shapes=[
            pltpu.VMEM((rows, gain.size), jnp.bfloat16),
        ],
        compiler_params=pltpu.CompilerParams(vmem_limit_bytes=8 * 2**20),
        name="expert_mlp",
    )(
        table,
        same,
        other,
        gain,
        experts,
        gates,
        in_vmem(w_gate),
        in_vmem(w_up),
        in_vmem(w_down),
    )


def gather_equal(x, axes, count):
    spread = jnp.broadcast_to(x[None], (count,) + x.shape)
    return lax.all_to_all(spread, axes, 0, 0, tiled=True)


def body(
    latent_cache,
    lengths,
    destination,
    queries,
    new_latent,
    residual,
    w_out,
    norm_gain,
    w_gate,
    w_up,
    w_down,
    experts,
    gate_weights,
):
    chips = lax.axis_size("chip")
    tp_width = lax.axis_size("tp")
    ranks = chips * 2
    chip_here = lax.axis_index("chip")
    core_here = lax.axis_index("core")
    tp_here = lax.axis_index("tp")
    rank_here = chip_here * 2 + core_here
    slot_count, positions, latent_all = latent_cache.shape
    heads_here, latent_width, column_count = w_out.shape
    step_count = queries.shape[1]
    block_rows = slot_count * step_count
    row_total = ranks * block_rows

    slots = jnp.tile(jnp.arange(slot_count, dtype=jnp.int32), ranks)
    request = jnp.arange(ranks * slot_count, dtype=jnp.int32)
    goes_to = destination * slot_count + slots
    source = jnp.sum(
        jnp.where(goes_to[None, :] == request[:, None], request[None, :], 0), axis=1
    )
    moved_len = jnp.sum(
        jnp.where(goes_to[None, :] == request[:, None], lengths[None, :], 0), axis=1
    )
    relative = (source // slot_count) ^ rank_here
    place = (
        (
            (relative & 1) * chips
            + ((relative >> 1) & 1) * (chips // 2)
            + (chips // 2 - 1 - (relative >> 2))
        )
        * slot_count
        + source % slot_count
    )
    served = jnp.sum(
        jnp.where(place[None, :] == request[:, None], request[None, :], 0), axis=1
    )
    table = jnp.concatenate(
        [place, moved_len, served, rank_here[None], tp_here[None]]
    ).astype(jnp.int32)
    with_kernels = (
        slot_count == 2
        and step_count == 2
        and chips == 8
        and tp_width == 2
        and (positions, heads_here, latent_width, column_count) == (32, 32, 512, 224)
    )
    near_cache = latent_cache
    if with_kernels:
        near_cache, near_queries, near_fresh = bring(latent_cache, queries, new_latent)
    wanted = [jnp.swapaxes(w_out, 1, 2), residual] if with_kernels else []
    parts, table, wanted = gather_relative(latent_cache, near_cache, table, wanted)
    own_gate = jnp.sum(jnp.where(experts == rank_here, gate_weights, 0.0), axis=2).reshape(
        row_total, 1
    )
    share = column_count // tp_width
    if with_kernels:
        w_columns, near_residual = wanted
        sent = weigh(table, parts, near_queries, near_fresh, latent_width)
        sent_same = gather_equal(sent, "chip", chips)
        head_partial, residual_rows, *expert_weights = project(
            table,
            parts,
            sent_same,
            swap_core(sent_same),
            near_residual,
            w_columns,
            (w_down[0],),
        )
    else:
        moved = jnp.concatenate(parts).reshape(ranks * slot_count, positions, latent_all)[place]
        position_range = jnp.arange(positions, dtype=jnp.int32)

        def inserted(base, fresh, length):
            for step_index in range(step_count):
                writing = position_range[None, :] == (length + step_index)[:, None]
                base = jnp.where(writing[:, :, None], fresh[:, step_index][:, None, :], base)
            return base

        own_first = rank_here * slot_count
        own_len = lax.dynamic_slice_in_dim(moved_len, own_first, slot_count, 0)
        own_cache = inserted(
            lax.dynamic_slice_in_dim(moved, own_first, slot_count, 0), new_latent, own_len
        )
        visible = (
            position_range[None, None, :]
            < (own_len[:, None] + jnp.arange(step_count, dtype=jnp.int32)[None, :] + 1)[:, :, None]
        )
        scores = (
            jnp.einsum("stha,spa->sthp", queries, own_cache, preferred_element_type=jnp.float32)
            * score_scale
        )
        scores = jnp.where(visible[:, :, None, :], scores, -1e30)
        highest = jnp.max(scores, axis=-1, keepdims=True)
        raised = jnp.exp(scores - highest)
        weights = (raised / jnp.sum(raised, axis=-1, keepdims=True)).astype(jnp.bfloat16)

        weight_count = block_rows * heads_here * positions
        fresh_count = block_rows * latent_width
        lane = 128
        sent = jnp.concatenate(
            [
                weights.reshape(weight_count // lane, lane),
                new_latent[..., :latent_width].reshape(fresh_count // lane, lane),
            ]
        )
        arrived = gather_equal(sent, ("chip", "core"), ranks)
        all_weights = arrived[:, : weight_count // lane].reshape(
            ranks * slot_count, step_count, heads_here, positions
        )
        all_fresh = arrived[:, weight_count // lane :].reshape(
            ranks * slot_count, step_count, latent_width
        )
        all_cache = inserted(moved[..., :latent_width], all_fresh, moved_len)
        attended = jnp.einsum(
            "gthp,gpl->gthl", all_weights, all_cache, preferred_element_type=jnp.float32
        ).astype(jnp.bfloat16)
        head_partial = jnp.dot(
            attended.reshape(row_total, heads_here * latent_width),
            w_out.reshape(heads_here * latent_width, column_count),
            preferred_element_type=jnp.float32,
        ).astype(jnp.bfloat16)
    if not with_kernels:
        residual_rows = residual.reshape(row_total, column_count)
    attn_cols = head_partial.astype(jnp.float32)
    for k in range(1, tp_width):
        attn_cols = attn_cols + swap_tp(head_partial, k).astype(jnp.float32)
    mixed = (residual_rows.astype(jnp.float32) + attn_cols).astype(
        jnp.bfloat16
    )

    same_core = gather_equal(mixed, "chip", chips)
    other_core = swap_core(same_core)
    if with_kernels:
        mine, theirs, own_columns = run_expert(
            table,
            same_core,
            other_core,
            norm_gain.reshape(norm_gain.size // 128, 128),
            jnp.transpose(experts, (1, 2, 0)),
            jnp.transpose(gate_weights, (1, 2, 0)),
            w_gate[0],
            w_up[0],
            *expert_weights,
            share,
        )
        leaving = (mine.astype(jnp.float32) + swap_core(theirs).astype(jnp.float32)).astype(
            jnp.bfloat16
        )
    else:
        first = jnp.where(core_here == 0, same_core, other_core)
        second = jnp.where(core_here == 0, other_core, same_core)
        rows_in = jnp.stack([first, second], axis=1).transpose(2, 0, 1, 3).reshape(row_total, -1)
        rows_wide = rows_in.astype(jnp.float32)
        inverse_rms = lax.rsqrt(jnp.mean(rows_wide * rows_wide, axis=-1, keepdims=True) + norm_eps)
        normed = (rows_wide * inverse_rms * norm_gain).astype(jnp.bfloat16)
        gate_proj = jnp.dot(normed, w_gate[0], preferred_element_type=jnp.float32)
        up_proj = jnp.dot(normed, w_up[0], preferred_element_type=jnp.float32)
        activated = (jax.nn.silu(gate_proj) * up_proj).astype(jnp.bfloat16)
        expert_terms = jnp.dot(activated, w_down[0], preferred_element_type=jnp.float32)
        terms = (
            (expert_terms * own_gate)
            .astype(jnp.bfloat16)
            .reshape(row_total, chips, 2, tp_width * share)
            .transpose(2, 1, 0, 3)
        )
        mine = lax.dynamic_index_in_dim(terms, core_here, 0, keepdims=False)
        theirs = lax.dynamic_index_in_dim(terms, 1 - core_here, 0, keepdims=False)
        chip_sum = (mine.astype(jnp.float32) + swap_core(theirs).astype(jnp.float32)).astype(
            jnp.bfloat16
        )
        leaving = (
            chip_sum.reshape(chips, row_total, tp_width, share)
            .transpose(0, 2, 1, 3)
            .reshape(chips * tp_width, row_total, share)
        )
    returned = lax.all_to_all(leaving, ("chip", "tp"), 0, 0, tiled=True)
    moe_part = jnp.sum(returned.astype(jnp.float32), axis=0)
    if not with_kernels:
        own_columns = lax.dynamic_slice_in_dim(mixed, tp_here * share, share, 1)
    return (
        (own_columns.astype(jnp.float32) + moe_part)
        .astype(jnp.bfloat16)
        .reshape(residual.shape[0], step_count, share)
    )


def solution(mesh):
    groups, ranks, tp_width = (mesh.shape[name] for name in ("groups", "dp", "tp"))
    split = Mesh(
        mesh.devices.reshape(groups, ranks // 2, 2, tp_width), ("groups", "chip", "core", "tp")
    )
    dp = ("chip", "core")
    placed = (
        P(("groups",) + dp, None, None),
        P("groups"),
        P("groups"),
        P(("groups",) + dp, None, "tp", None),
        P(("groups",) + dp, None, None),
        P("groups", None, dp),
        P("tp", None, dp),
        P(),
        P(dp, None, "tp"),
        P(dp, None, "tp"),
        P(dp, "tp", None),
        P("groups", None, None),
        P("groups", None, None),
    )
    return jax.shard_map(
        body,
        mesh=split,
        in_specs=placed,
        out_specs=P("groups", None, dp + ("tp",)),
        check_vma=False,
    )
```
